32 devices in a mesh: flow: 16 (over z, y, core), tm: 2 (over x).
Axes of the slice: x: 2, y: 2, z: 4, core: 2. Of those that a mesh axis runs over, the one named last changes fastest.
Arguments:
- traffic: float32 [61440, 256], P('flow', 'tm'), may hold values from -15 to 15
- thresholds: float32 [61440], P('flow'), may hold values from 0.5 to 2
- flow_factor: float32 [61440, 64], P(('flow', 'tm')), may hold values from -6 to 6
- time_factor: float32 [256, 64], P(('tm', 'flow')), may hold values from -3 to 3
Outputs:
- anomaly: float32 [61440, 256], P('flow', 'tm')
- flow_new: float32 [61440, 64], P(('flow', 'tm'))
- time_new: float32 [256, 64], P(('tm', 'flow'))
The draws below stay inside these ranges and needn't reach their ends.
All inputs are finite; a program needn't handle non-finite values.
Results may differ from the reference program's by a relative error of at most 0.0003.
Values sent between devices are 32-bit elements; how exact they have to be, the bound alone decides.
A program may use at most 64 MiB of HBM per device.

```python
import math
import jax
import jax.numpy as jnp
from jax import lax

FLOW_DEV = 3840
RANK = 64
ITERS = 4
FLOWS = 61440
BINS = 256
N_FLOW = 16


def shared_truth(key):
    key_left, key_right = jax.random.split(key)
    left_true = jnp.clip(jax.random.normal(key_left, (FLOWS, RANK), jnp.float32), -5.0, 5.0)
    right_true = jnp.clip(jax.random.normal(key_right, (BINS, RANK), jnp.float32), -5.0, 5.0)
    return (left_true, right_true)


def draw_traffic(key, part):
    left_true, right_true = shared_truth(key)
    key = jax.random.fold_in(key, 11)
    key_mask, key_size, key_sign, key_noise = jax.random.split(key, 4)
    low_rank = jnp.clip(jnp.dot(left_true, right_true.T) * RANK ** (-0.5), -6.0, 6.0)
    hits = jax.random.bernoulli(key_mask, 0.04, (FLOWS, BINS)).astype(jnp.float32)
    sizes = jax.random.uniform(key_size, (FLOWS, BINS), jnp.float32, 3.0, 8.0)
    signs = jnp.where(jax.random.bernoulli(key_sign, 0.5, (FLOWS, BINS)), 1.0, -1.0)
    noise = 0.15 * jnp.clip(jax.random.normal(key_noise, (FLOWS, BINS), jnp.float32), -4.0, 4.0)
    return (low_rank + hits * sizes * signs + noise).astype(jnp.float32)


def draw_flow_factor(key, part):
    left_true, right_true = shared_truth(key)
    key = jax.random.fold_in(key, 23)
    noise = jnp.clip(jax.random.normal(key, (FLOWS, RANK), jnp.float32), -5.0, 5.0)
    rising = 1.0 + 2.0 * jnp.arange(FLOWS, dtype=jnp.float32)[:, None] / FLOWS
    return ((left_true * rising + 0.3 * noise) * RANK ** (-0.25)).astype(jnp.float32)


def draw_time_factor(key, part):
    left_true, right_true = shared_truth(key)
    key = jax.random.fold_in(key, 37)
    noise = jnp.clip(jax.random.normal(key, (BINS, RANK), jnp.float32), -5.0, 5.0)
    return ((right_true + 0.3 * noise) * RANK ** (-0.25)).astype(jnp.float32)


def level_of(own_key, dims, pieces, least, high):
    level, own = 1.0, jax.random.fold_in(own_key, 6)
    for axis_at, blocks in pieces:
        steps = jnp.exp(jax.random.uniform(jax.random.fold_in(own, axis_at), (blocks,), jnp.float32, least / len(pieces), high / len(pieces)))
        level = level * jnp.repeat(steps, dims[axis_at] // blocks).reshape([-1 if axis == axis_at else 1 for axis in range(len(dims))])
    return level


def setup_inputs(seed: int = 0) -> dict:
    streams_of = jax.random.split(jax.random.key(seed), 5)
    traffic = draw_traffic(jax.random.fold_in(streams_of[4], 71), 0)
    thresholds = jnp.clip(jnp.exp(math.log(2.0) - 1.3862944 * jax.random.uniform(streams_of[1], (FLOWS,), jnp.float32) ** level_of(streams_of[1], (FLOWS,), ((0, 16),), -0.2, 0.2)), 0.5, 2.0)
    flow_factor = draw_flow_factor(jax.random.fold_in(streams_of[4], 71), 0)
    time_factor = draw_time_factor(jax.random.fold_in(streams_of[4], 71), 0)
    return {"traffic": traffic, "thresholds": thresholds, "flow_factor": flow_factor, "time_factor": time_factor}


step_size = 0.5
ridge_term = 1.0

def soft_split(difference, limits):
    anomaly = jnp.sign(difference) * jnp.maximum(jnp.abs(difference) - limits, 0.0)
    return (anomaly, difference - anomaly)

def precondition(gradient, gram_matrix):
    factor_low = jnp.linalg.cholesky(gram_matrix)
    return jax.scipy.linalg.cho_solve((factor_low, True), gradient.T).T

def reference(traffic, thresholds, flow_factor, time_factor):
    highest = lax.Precision.HIGHEST
    matrix_blocks = traffic.reshape(N_FLOW, FLOW_DEV, BINS)
    limit_blocks = thresholds.reshape(N_FLOW, FLOW_DEV, 1)
    identity = jnp.eye(RANK, dtype=jnp.float32)
    anomaly = jnp.zeros_like(traffic)
    for rounds in range(ITERS):
        factor_blocks = flow_factor.reshape(N_FLOW, FLOW_DEV, RANK)

        def one_block(total, item):
            matrix, factor_rows, limits = item
            low_rank = jnp.dot(factor_rows.astype(jnp.float32), time_factor.T.astype(jnp.float32), precision=highest, preferred_element_type=jnp.float32)
            found, residual = soft_split(matrix - low_rank, limits)
            grad_rows = jnp.dot(residual.astype(jnp.float32), time_factor.astype(jnp.float32), precision=highest, preferred_element_type=jnp.float32)
            total = total + jnp.dot(residual.T.astype(jnp.float32), factor_rows.astype(jnp.float32), precision=highest, preferred_element_type=jnp.float32)
            return (total, (found, grad_rows))
        grad_time, (found_all, grad_flow) = lax.scan(one_block, jnp.zeros((BINS, RANK), jnp.float32), (matrix_blocks, factor_blocks, limit_blocks))
        anomaly = found_all.reshape(FLOWS, BINS)
        grad_flow = grad_flow.reshape(FLOWS, RANK) - ridge_term * flow_factor
        grad_time = grad_time - ridge_term * time_factor
        gram_flow = jnp.dot(flow_factor.T.astype(jnp.float32), flow_factor.astype(jnp.float32), precision=highest, preferred_element_type=jnp.float32) + ridge_term * identity
        gram_time = jnp.dot(time_factor.T.astype(jnp.float32), time_factor.astype(jnp.float32), precision=highest, preferred_element_type=jnp.float32) + ridge_term * identity
        flow_next = flow_factor + step_size * precondition(grad_flow, gram_time)
        time_factor = time_factor + step_size * precondition(grad_time, gram_flow)
        flow_factor = flow_next
    return (anomaly, flow_factor, time_factor)
```

```python
import functools
import jax
import jax.numpy as jnp
from jax import lax
from jax.experimental import pallas as pl
from jax.experimental.pallas import tpu as pltpu
from jax.sharding import PartitionSpec as P

ITERS = 4
STEP = 0.5
RIDGE = 1.0
LANES = 128
F32 = jnp.float32
BF16 = jnp.bfloat16
MESH = pl.DeviceIdType.MESH


def exact(a, b, dims):
    return lax.dot_general(
        a, b, (dims, ((), ())), precision=lax.Precision.HIGHEST, preferred_element_type=F32
    )


def quick(a, b, dims=((1,), (0,))):
    return lax.dot_general(a, b, (dims, ((), ())), preferred_element_type=F32)


def halves(x):
    high = x.astype(BF16)
    return high, (x - high.astype(F32)).astype(BF16)


def iota(shape, dim):
    return lax.broadcasted_iota(jnp.int32, shape, dim)


class Total:
    def __init__(self, place, source, first, second, out, sems):
        self.place, self.source, self.first, self.second, self.out = place, source, first, second, out
        self.s1, self.r1, self.s2, self.r2, self.s3, self.r3 = sems
        self.c = source.shape[0] // place.n1

    def rows(self, member):
        return pl.ds(pl.multiple_of(member * self.c, 8), self.c)

    def copy1(self, d):
        p = self.place
        peer = lax.rem(p.g1 + d, p.n1)
        return pltpu.make_async_remote_copy(
            src_ref=self.source.at[self.rows(peer)], dst_ref=self.first.at[d],
            send_sem=self.s1.at[d], recv_sem=self.r1.at[d],
            device_id=p.device(peer, p.g2), device_id_type=MESH)

    def copy2(self, d, slot, landing):
        p = self.place
        peer = lax.rem(p.g2 + d, p.n2)
        who = peer if landing else p.g2
        return pltpu.make_async_remote_copy(
            src_ref=self.second.at[slot, who], dst_ref=self.second.at[slot, who],
            send_sem=self.s2.at[d], recv_sem=self.r2.at[slot, who],
            device_id=p.device(p.g1, peer), device_id_type=MESH)

    def copy3(self, d, landing):
        p = self.place
        peer = lax.rem(p.g1 + d, p.n1)
        who = peer if landing else p.g1
        return pltpu.make_async_remote_copy(
            src_ref=self.out.at[self.rows(who)], dst_ref=self.out.at[self.rows(who)],
            send_sem=self.s3.at[d], recv_sem=self.r3.at[who],
            device_id=p.device(peer, p.g2), device_id_type=MESH)

    def begin(self):
        for d in range(1, self.place.n1):
            self.copy1(d).start()

    def middle(self, slot):
        p = self.place
        total = self.source[self.rows(p.g1), :]
        for d in range(1, p.n1):
            self.copy1(d).wait_recv()
            total = total + self.first[d]
        self.second[slot, p.g2] = total
        p.others2(lambda d: self.copy2(d, slot, False).start())
        for d in range(1, p.n1):
            self.copy1(d).wait_send()

    def last(self, slot):
        p = self.place
        p.others2(lambda d: self.copy2(d, slot, True).wait_recv())
        p.others2(lambda d: self.copy2(d, slot, False).wait_send())
        if p.n2 <= 8:
            total = self.second[slot, 0]
            for j in range(1, p.n2):
                total = total + self.second[slot, j]
        else:
            total = lax.fori_loop(
                1, p.n2, lambda j, t: t + self.second[slot, j], self.second[slot, 0])
        self.out[self.rows(p.g1), :] = total
        for d in range(1, p.n1):
            self.copy3(d, False).start()

    def end(self):
        p = self.place
        for d in range(1, p.n1):
            self.copy3(d, True).wait_recv()
        for d in range(1, p.n1):
            self.copy3(d, False).wait_send()


class Place:
    def __init__(self, n_flow, n_tm):
        self.fl, self.tl = 4, 2
        self.n1 = self.fl * self.tl
        self.th = n_tm // self.tl
        self.n2 = n_flow // self.fl * self.th
        self.n_flow, self.n_tm = n_flow, n_tm
        self.flow, self.tm = lax.axis_index("flow"), lax.axis_index("tm")
        self.g1 = lax.rem(self.flow, self.fl) * self.tl + lax.rem(self.tm, self.tl)
        self.g2 = lax.div(self.flow, self.fl) * self.th + lax.div(self.tm, self.tl)

    def device(self, g1, g2):
        return (
            lax.div(g2, self.th) * self.fl + lax.div(g1, self.tl),
            lax.rem(g2, self.th) * self.tl + lax.rem(g1, self.tl),
        )

    def others2(self, do):
        if self.n2 <= 8:
            for d in range(1, self.n2):
                do(d)
        else:
            lax.fori_loop(1, self.n2, lambda d, _: (do(d), 0)[1], 0)


def pivot(a, k, rank):
    lane, row = iota(a.shape, 1), iota(a.shape, 0)
    left = lane < rank
    own = jnp.where(left, lane, lane - rank) == k
    col = jnp.where(left, a[:, k : k + 1], a[:, rank + k : rank + k + 1])
    line = jnp.where(own[:1], 1.0, a[k : k + 1, :]) / col[k : k + 1, :]
    return jnp.where(own | (row == k), 0.0, a) - jnp.where(row == k, -1.0, col) * line


def kernel(
    n_flow, n_tm, traffic, thr, flow_ref, time_ref, anom_out, flow_out, time_out,
    held, whole, wide, u2, ul, rhi, rlo, vt, vcat, acc, gacc, stage, ug, upack,
    gsrc, gfirst, gsecond, gout, hsrc, hfirst, hsecond, hout,
    gs1, gr1, gs2, gr2, gs3, gr3, hs1, hr1, hs2, hr2, hs3, hr3,
    tsend, trecv, tlocal, usend, urecv,
):
    p = Place(n_flow, n_tm)
    rank = vt.shape[0]
    bins = vt.shape[1]
    rows = u2.shape[0]
    block = bins // n_tm
    half = rows // 2
    nb = bins // LANES
    tile = rows // 4 if rows % 64 == 0 else rows
    tiles = rows // tile
    grad = Total(p, gsrc, gfirst, gsecond, gout, (gs1, gr1, gs2, gr2, gs3, gr3))
    gram = Total(p, hsrc, hfirst, hsecond, hout, (hs1, hr1, hs2, hr2, hs3, hr3))

    barrier = pltpu.get_barrier_semaphore()
    for d in range(1, p.n1):
        pl.semaphore_signal(barrier, 1, device_id=p.device(lax.rem(p.g1 + d, p.n1), p.g2), device_id_type=MESH)
    p.others2(lambda d: pl.semaphore_signal(
        barrier, 1, device_id=p.device(p.g1, lax.rem(p.g2 + d, p.n2)), device_id_type=MESH))
    for d in range(1, n_tm):
        pl.semaphore_signal(barrier, 1, device_id=(p.flow, lax.rem(p.tm + d, n_tm)), device_id_type=MESH)

    def own_rows(who):
        return pl.ds(pl.multiple_of(who * rows, 8), rows)

    def send_traffic(d):
        peer = lax.rem(p.tm + d, n_tm)
        return pltpu.make_async_remote_copy(
            src_ref=traffic.at[own_rows(peer)], dst_ref=held.at[p.tm],
            send_sem=tsend.at[d], recv_sem=trecv.at[p.tm],
            device_id=(p.flow, peer), device_id_type=MESH)

    def get_traffic(d):
        peer = lax.rem(p.tm + d, n_tm)
        return pltpu.make_async_remote_copy(
            src_ref=traffic.at[own_rows(peer)], dst_ref=held.at[peer],
            send_sem=tsend.at[d], recv_sem=trecv.at[peer],
            device_id=(p.flow, peer), device_id_type=MESH)

    def send_flow(d, landing):
        peer = lax.rem(p.tm + d, n_tm)
        who = peer if landing else p.tm
        return pltpu.make_async_remote_copy(
            src_ref=upack, dst_ref=ug.at[who], send_sem=usend.at[d], recv_sem=urecv.at[who],
            device_id=(p.flow, peer), device_id_type=MESH)

    local = [
        pltpu.make_async_copy(traffic, whole, tlocal.at[0]),
        pltpu.make_async_copy(traffic.at[own_rows(p.tm)], held.at[p.tm], tlocal.at[1]),
    ]
    for c in local:
        c.start()

    stage[...] = jnp.zeros_like(stage)
    share = time_ref.shape[0]
    mine = p.tm * n_flow + p.flow
    at = mine * share
    if share % 8 == 0:
        at = pl.multiple_of(at, 8)
    stage[pl.ds(at, share), :rank] = time_ref[...]
    turned = stage[...].T[:rank]
    for j in range(nb):
        gsrc[rank * j : rank * (j + 1), :] = turned[:, LANES * j : LANES * (j + 1)]

    pl.semaphore_wait(barrier, p.n1 + p.n2 + n_tm - 3)
    grad.begin()
    for d in range(1, n_tm):
        send_traffic(d).start()

    left = iota((tile, LANES), 1) < rank

    def keep_flow(at, x):
        u2[at, :] = x
        high = x.astype(BF16)
        high32 = high.astype(F32)
        hl = jnp.where(left, high32, x - high32).astype(BF16)
        ul[at, :LANES] = hl
        ul[at, LANES:] = high
        gacc[...] += quick(hl, hl, ((0,), (0,)))

    def tile_rows(i):
        return pl.ds(pl.multiple_of(i * tile, 16), tile)

    def send_gram():
        hsrc[...] = gacc[:rank, :] + gacc[rank:, :]
        gram.begin()

    gacc[...] = jnp.zeros_like(gacc)

    def start_tile(i, _):
        x = flow_ref[tile_rows(i), :]
        keep_flow(tile_rows(i), jnp.concatenate([x, x], axis=1))
        return 0

    lax.fori_loop(0, tiles, start_tile, 0)
    send_gram()
    grad.middle(0)
    for i in range(thr.shape[0]):
        wide[LANES * i : LANES * (i + 1), :] = jnp.broadcast_to(thr[i : i + 1, :], (LANES, LANES)).T
    grad.last(0)

    def keep_time(x):
        vt[...] = x
        high, low = halves(x)
        vcat[:rank, :] = high
        vcat[rank : 2 * rank, :] = high
        vcat[2 * rank : 3 * rank, :] = low
        vcat[3 * rank :, :] = jnp.zeros_like(low)

    def time_sum():
        return jnp.concatenate([gout[rank * j : rank * (j + 1), :] for j in range(nb)], axis=1)

    grad.end()
    keep_time(time_sum())
    for c in local:
        c.wait()
    for d in range(1, n_tm):
        get_traffic(d).wait_recv()
        send_traffic(d).wait_send()

    def step(it, _):
        slot, next_slot = lax.rem(it, 2), lax.rem(it + 1, 2)
        final = it == ITERS - 1
        acc[...] = jnp.zeros_like(acc)

        def first_tile(i, _):
            at = tile_rows(i)
            low_rank = quick(ul[at, :], vcat[...])
            limit = wide[pl.ds(pl.multiple_of(p.tm * rows + i * tile, 8), tile), :block]
            parts = []
            for j in range(n_tm):
                diff = held[j, at, :] - low_rank[:, block * j : block * (j + 1)]
                rest = jnp.minimum(jnp.maximum(diff, -limit), limit)
                parts.append(rest)

                @pl.when(final & (p.tm == j))
                def _():
                    anom_out[pl.ds(pl.multiple_of(p.tm * rows + i * tile, 8), tile), :] = diff - rest

            rest = jnp.concatenate(parts, axis=1)
            high, low = halves(rest)
            rhi[at, :] = high
            rlo[at, :] = low
            hl = ul[at, :LANES]
            acc[...] += quick(hl, high, ((0,), (0,))) + quick(hl, low, ((0,), (0,)))
            return 0

        lax.fori_loop(0, tiles // 2, first_tile, 0)
        gram.middle(slot)
        lax.fori_loop(tiles // 2, tiles, first_tile, 0)
        for j in range(nb):
            cols = slice(LANES * j, LANES * (j + 1))
            gsrc[rank * j : rank * (j + 1), :] = acc[:rank, cols] + acc[rank:, cols]
        grad.begin()
        gram.last(slot)

        now = vt[...]
        gram_time = exact(now, jnp.concatenate([now, now], axis=0), ((1,), (1,)))
        gram.end()
        gf = hout[...]
        gram_flow = gf + pltpu.roll(gf, rank, 1)
        lane, row = iota(gf.shape, 1), iota(gf.shape, 0)
        eye = jnp.where((lane == row) | (lane == row + rank), RIDGE, 0.0)
        a = jnp.where(lane < rank, gram_time, gram_flow) + eye
        for k in range(rank):
            if k == rank // 2:
                grad.middle(next_slot)
            if k == 3 * rank // 4:
                grad.last(next_slot)
            a = pivot(a, k, rank)
        other = pltpu.roll(a, rank, 1)
        inv_time2 = STEP * jnp.where(lane < rank, a, other)
        inv_flow = STEP * other[:, :rank]
        wt = exact(inv_time2[:, :rank], now, ((1,), (0,)))
        w2 = jnp.concatenate([wt, wt], axis=0).T
        whi, wlo = halves(w2)
        wcat = jnp.concatenate([whi, wlo], axis=1)
        phi, plo = halves(inv_time2)
        pcat = jnp.concatenate([phi, phi, plo, jnp.zeros_like(plo)], axis=0)
        gacc[...] = jnp.zeros_like(gacc)

        def second_tile(i, _):
            at = tile_rows(i)
            o = quick(rhi[at, :], wcat)
            o = o[:, :LANES] + o[:, LANES:] + quick(rlo[at, :], whi) - quick(ul[at, :], pcat)
            keep_flow(at, u2[at, :] + o)
            return 0

        lax.fori_loop(0, tiles, second_tile, 0)

        @pl.when(jnp.logical_not(final))
        def _():
            send_gram()

        @pl.when(it == ITERS - 2)
        def _():
            upack[...] = jnp.where(iota((half, LANES), 1) < rank, u2[:half, :], u2[half:, :])
            for d in range(1, n_tm):
                send_flow(d, False).start()

        @pl.when(final)
        def _():
            mine = jnp.zeros((rank, block), F32)
            for j in range(n_tm):
                mine = jnp.where(p.tm == j, now[:, block * j : block * (j + 1)], mine)
            vhi, vlo = halves(mine)
            zero = jnp.zeros_like(vhi)
            ops = (
                (jnp.concatenate([vhi, zero, vhi, zero], axis=0), jnp.concatenate([vlo, zero], axis=0)),
                (jnp.concatenate([zero, vhi, zero, vhi], axis=0), jnp.concatenate([zero, vlo], axis=0)),
            )
            for d in range(1, n_tm):
                send_flow(d, True).wait_recv()
                peer = lax.rem(p.tm + d, n_tm)
                high, low = halves(ug[peer])
                both = jnp.concatenate([high, low], axis=1)
                for h in range(2):
                    at = pl.ds(pl.multiple_of(peer * rows + h * half, 8), half)
                    low_rank = quick(both, ops[h][0]) + quick(high, ops[h][1])
                    diff = whole[at, :] - low_rank
                    limit = wide[at, :block]
                    anom_out[at, :] = diff - jnp.minimum(jnp.maximum(diff, -limit), limit)
                send_flow(d, False).wait_send()

        grad.end()
        keep_time(now + exact(inv_flow, time_sum() - now, ((1,), (0,))))
        return 0

    lax.fori_loop(0, ITERS, step, 0)
    flow_out[...] = u2[:, :rank]
    stage[...] = jnp.concatenate([vt[...], vt[...]], axis=0).T
    time_out[...] = stage[pl.ds(at, share), :rank]


def solution(mesh):
    n_flow, n_tm = mesh.shape["flow"], mesh.shape["tm"]

    def body(traffic, thresholds, flow_factor, time_factor):
        all_rows, block = traffic.shape
        rows, rank = flow_factor.shape
        bins = block * n_tm
        n1 = 8
        n2 = n_flow * n_tm // n1
        gr, hr = rank * bins // LANES, rank
        thr = thresholds.reshape(all_rows // LANES, LANES)
        vmem = pl.BlockSpec(memory_space=pltpu.VMEM)
        dma = pltpu.SemaphoreType.DMA
        sums = []
        sems = []
        for r in (gr, hr):
            c = r // n1
            sums += [
                pltpu.VMEM((r, LANES), F32), pltpu.VMEM((n1, c, LANES), F32),
                pltpu.VMEM((2, n2, c, LANES), F32), pltpu.VMEM((r, LANES), F32),
            ]
            sems += [dma((n1,)), dma((n1,)), dma((n2,)), dma((2, n2)), dma((n1,)), dma((n1,))]
        return pl.pallas_call(
            functools.partial(kernel, n_flow, n_tm),
            out_shape=(
                jax.ShapeDtypeStruct((all_rows, block), F32),
                jax.ShapeDtypeStruct((rows, rank), F32),
                jax.ShapeDtypeStruct(time_factor.shape, F32),
            ),
            in_specs=[pl.BlockSpec(memory_space=pl.ANY), vmem, vmem, vmem],
            out_specs=(vmem, vmem, vmem),
            scratch_shapes=[
                pltpu.VMEM((n_tm, rows, block), F32),
                pltpu.VMEM((all_rows, block), F32),
                pltpu.VMEM((all_rows, LANES), F32),
                pltpu.VMEM((rows, LANES), F32),
                pltpu.VMEM((rows, 2 * LANES), BF16),
                pltpu.VMEM((rows, bins), BF16),
                pltpu.VMEM((rows, bins), BF16),
                pltpu.VMEM((rank, bins), F32),
                pltpu.VMEM((4 * rank, bins), BF16),
                pltpu.VMEM((2 * rank, bins), F32),
                pltpu.VMEM((2 * rank, LANES), F32),
                pltpu.VMEM((bins, LANES), F32),
                pltpu.VMEM((n_tm, rows // 2, LANES), F32),
                pltpu.VMEM((rows // 2, LANES), F32),
            ] + sums + sems + [
                dma((n_tm,)), dma((n_tm,)), dma((2,)), dma((n_tm,)), dma((n_tm,)),
            ],
            compiler_params=pltpu.CompilerParams(
                collective_id=0, has_side_effects=True, vmem_limit_bytes=56 * 1024 * 1024
            ),
            name="pca",
        )(traffic, thr, flow_factor, time_factor)

    return jax.shard_map(
        body,
        mesh=mesh,
        in_specs=(P("flow", "tm"), P("flow"), P(("flow", "tm"), None), P(("tm", "flow"), None)),
        out_specs=(P("flow", "tm"), P(("flow", "tm"), None), P(("tm", "flow"), None)),
        check_vma=False,
    )
```

```python
import functools
import jax
import jax.numpy as jnp
from jax import lax
from jax.experimental import pallas as pl
from jax.experimental.pallas import tpu as pltpu
from jax.sharding import PartitionSpec as P

ITERS = 4
STEP = 0.5
RIDGE = 1.0
LANES = 128
FIRST_AT = 24
SECOND_AT = 56
F32 = jnp.float32
BF16 = jnp.bfloat16
MESH = pl.DeviceIdType.MESH


def exact(a, b, dims):
    return lax.dot_general(
        a, b, (dims, ((), ())), precision=lax.Precision.HIGHEST, preferred_element_type=F32
    )


def quick(a, b, dims=((1,), (0,))):
    return lax.dot_general(a, b, (dims, ((), ())), preferred_element_type=F32)


def halves(x):
    high = x.astype(BF16)
    return high, (x - high.astype(F32)).astype(BF16)


def iota(shape, dim):
    return lax.broadcasted_iota(jnp.int32, shape, dim)


class Total:
    def __init__(self, place, source, first, second, out, sems):
        self.place, self.source, self.first, self.second, self.out = place, source, first, second, out
        self.s1, self.r1, self.s2, self.r2, self.s3, self.r3 = sems
        self.c = source.shape[0] // place.n1

    def rows(self, member):
        return pl.ds(pl.multiple_of(member * self.c, 8), self.c)

    def copy1(self, d):
        p = self.place
        peer = lax.rem(p.g1 + d, p.n1)
        return pltpu.make_async_remote_copy(
            src_ref=self.source.at[self.rows(peer)], dst_ref=self.first.at[d],
            send_sem=self.s1.at[d], recv_sem=self.r1.at[d],
            device_id=p.device(peer, p.g2), device_id_type=MESH)

    def copy2(self, d, slot, landing):
        p = self.place
        peer = lax.rem(p.g2 + d, p.n2)
        who = peer if landing else p.g2
        return pltpu.make_async_remote_copy(
            src_ref=self.second.at[slot, who], dst_ref=self.second.at[slot, who],
            send_sem=self.s2.at[d], recv_sem=self.r2.at[slot, who],
            device_id=p.device(p.g1, peer), device_id_type=MESH)

    def copy3(self, d, landing):
        p = self.place
        peer = lax.rem(p.g1 + d, p.n1)
        who = peer if landing else p.g1
        return pltpu.make_async_remote_copy(
            src_ref=self.out.at[self.rows(who)], dst_ref=self.out.at[self.rows(who)],
            send_sem=self.s3.at[d], recv_sem=self.r3.at[who],
            device_id=p.device(peer, p.g2), device_id_type=MESH)

    def begin(self):
        for d in range(1, self.place.n1):
            self.copy1(d).start()

    def middle(self, slot):
        p = self.place
        total = self.source[self.rows(p.g1), :]
        for d in range(1, p.n1):
            self.copy1(d).wait_recv()
            total = total + self.first[d]
        self.second[slot, p.g2] = total
        p.others2(lambda d: self.copy2(d, slot, False).start())
        for d in range(1, p.n1):
            self.copy1(d).wait_send()

    def last(self, slot):
        p = self.place
        p.others2(lambda d: self.copy2(d, slot, True).wait_recv())
        p.others2(lambda d: self.copy2(d, slot, False).wait_send())
        if p.n2 <= 8:
            total = self.second[slot, 0]
            for j in range(1, p.n2):
                total = total + self.second[slot, j]
        else:
            total = lax.fori_loop(
                1, p.n2, lambda j, t: t + self.second[slot, j], self.second[slot, 0])
        self.out[self.rows(p.g1), :] = total
        for d in range(1, p.n1):
            self.copy3(d, False).start()

    def end(self):
        p = self.place
        for d in range(1, p.n1):
            self.copy3(d, True).wait_recv()
        for d in range(1, p.n1):
            self.copy3(d, False).wait_send()


class Place:
    def __init__(self, n_flow, n_tm):
        self.fl, self.tl = 4, 2
        self.n1 = self.fl * self.tl
        self.th = n_tm // self.tl
        self.n2 = n_flow // self.fl * self.th
        self.n_flow, self.n_tm = n_flow, n_tm
        self.flow, self.tm = lax.axis_index("flow"), lax.axis_index("tm")
        self.g1 = lax.rem(self.flow, self.fl) * self.tl + lax.rem(self.tm, self.tl)
        self.g2 = lax.div(self.flow, self.fl) * self.th + lax.div(self.tm, self.tl)

    def device(self, g1, g2):
        return (
            lax.div(g2, self.th) * self.fl + lax.div(g1, self.tl),
            lax.rem(g2, self.th) * self.tl + lax.rem(g1, self.tl),
        )

    def others2(self, do):
        if self.n2 <= 8:
            for d in range(1, self.n2):
                do(d)
        else:
            lax.fori_loop(1, self.n2, lambda d, _: (do(d), 0)[1], 0)


def pivot(a, k, rank):
    lane, row = iota(a.shape, 1), iota(a.shape, 0)
    left = lane < rank
    own = jnp.where(left, lane, lane - rank)
    first, second = own == k, own == k + 1
    col = jnp.where(left, a[:, k : k + 1], a[:, rank + k : rank + k + 1])
    col_next = jnp.where(left, a[:, k + 1 : k + 2], a[:, rank + k + 1 : rank + k + 2])
    p, q, s = col[k : k + 1, :], col[k + 1 : k + 2, :], col_next[k + 1 : k + 2, :]
    scale = 1.0 / (p * s - q * q)
    line = jnp.where(first[:1], 1.0, jnp.where(second[:1], 0.0, a[k : k + 1, :]))
    line_next = jnp.where(first[:1], 0.0, jnp.where(second[:1], 1.0, a[k + 1 : k + 2, :]))
    out = (s * scale) * line - (q * scale) * line_next
    out_next = (p * scale) * line_next - (q * scale) * line
    col = jnp.where(row == k, -1.0, jnp.where(row == k + 1, 0.0, col))
    col_next = jnp.where(row == k, 0.0, jnp.where(row == k + 1, -1.0, col_next))
    rest = jnp.where(first | second | (row == k) | (row == k + 1), 0.0, a)
    return rest - col * out - col_next * out_next


def kernel(
    n_flow, n_tm, traffic, thr, flow_ref, time_ref, anom_out, flow_out, time_out,
    held, whole, wide, u2, ul, rhi, rlo, vt, vcat, acc, gacc, stage, ug, upack,
    gsrc, gfirst, gsecond, gout, hsrc, hfirst, hsecond, hout,
    gs1, gr1, gs2, gr2, gs3, gr3, hs1, hr1, hs2, hr2, hs3, hr3,
    tsend, trecv, tlocal, usend, urecv, asend,
    found, wcat, pcat, inv_flow,
):
    p = Place(n_flow, n_tm)
    rank = vt.shape[0]
    bins = vt.shape[1]
    rows = u2.shape[0]
    block = bins // n_tm
    half = rows // 2
    nb = bins // LANES
    tile = rows // 4 if rows % 64 == 0 else rows
    tiles = rows // tile
    grad = Total(p, gsrc, gfirst, gsecond, gout, (gs1, gr1, gs2, gr2, gs3, gr3))
    gram = Total(p, hsrc, hfirst, hsecond, hout, (hs1, hr1, hs2, hr2, hs3, hr3))

    barrier = pltpu.get_barrier_semaphore()
    for d in range(1, p.n1):
        pl.semaphore_signal(barrier, 1, device_id=p.device(lax.rem(p.g1 + d, p.n1), p.g2), device_id_type=MESH)
    p.others2(lambda d: pl.semaphore_signal(
        barrier, 1, device_id=p.device(p.g1, lax.rem(p.g2 + d, p.n2)), device_id_type=MESH))
    for d in range(1, n_tm):
        pl.semaphore_signal(barrier, 1, device_id=(p.flow, lax.rem(p.tm + d, n_tm)), device_id_type=MESH)

    def own_rows(who):
        return pl.ds(pl.multiple_of(who * rows, 8), rows)

    def send_traffic(d):
        peer = lax.rem(p.tm + d, n_tm)
        return pltpu.make_async_remote_copy(
            src_ref=traffic.at[own_rows(peer)], dst_ref=held.at[p.tm],
            send_sem=tsend.at[d], recv_sem=trecv.at[p.tm],
            device_id=(p.flow, peer), device_id_type=MESH)

    def get_traffic(d):
        peer = lax.rem(p.tm + d, n_tm)
        return pltpu.make_async_remote_copy(
            src_ref=traffic.at[own_rows(peer)], dst_ref=held.at[peer],
            send_sem=tsend.at[d], recv_sem=trecv.at[peer],
            device_id=(p.flow, peer), device_id_type=MESH)

    def send_found(who):
        return pltpu.make_async_copy(found.at[own_rows(who)], anom_out.at[own_rows(who)], asend.at[who])

    def send_flow(d, landing):
        peer = lax.rem(p.tm + d, n_tm)
        who = peer if landing else p.tm
        return pltpu.make_async_remote_copy(
            src_ref=upack, dst_ref=ug.at[who], send_sem=usend.at[d], recv_sem=urecv.at[who],
            device_id=(p.flow, peer), device_id_type=MESH)

    local = [
        pltpu.make_async_copy(traffic, whole, tlocal.at[0]),
        pltpu.make_async_copy(traffic.at[own_rows(p.tm)], held.at[p.tm], tlocal.at[1]),
    ]
    for c in local:
        c.start()

    stage[...] = jnp.zeros_like(stage)
    share = time_ref.shape[0]
    mine = p.tm * n_flow + p.flow
    at = mine * share
    if share % 8 == 0:
        at = pl.multiple_of(at, 8)
    stage[pl.ds(at, share), :rank] = time_ref[...]
    turned = stage[...].T[:rank]
    for j in range(nb):
        gsrc[rank * j : rank * (j + 1), :] = turned[:, LANES * j : LANES * (j + 1)]

    pl.semaphore_wait(barrier, p.n1 + p.n2 + n_tm - 3)
    grad.begin()
    for d in range(1, n_tm):
        send_traffic(d).start()

    left = iota((tile, LANES), 1) < rank

    def keep_flow(at, x):
        u2[at, :] = x
        high = x.astype(BF16)
        high32 = high.astype(F32)
        hl = jnp.where(left, high32, x - high32).astype(BF16)
        ul[at, :LANES] = hl
        ul[at, LANES:] = high
        gacc[...] += quick(hl, hl, ((0,), (0,)))

    def tile_rows(i):
        return pl.ds(pl.multiple_of(i * tile, 16), tile)

    def send_gram():
        hsrc[...] = gacc[:rank, :] + gacc[rank:, :]
        gram.begin()

    gacc[...] = jnp.zeros_like(gacc)

    u2[...] = jnp.concatenate([flow_ref[...], flow_ref[...]], axis=0).T

    def start_tile(i, _):
        keep_flow(tile_rows(i), u2[tile_rows(i), :])
        return 0

    lax.fori_loop(0, tiles, start_tile, 0)
    send_gram()
    grad.middle(0)
    for i in range(thr.shape[0]):
        wide[LANES * i : LANES * (i + 1), :] = jnp.broadcast_to(thr[i : i + 1, :], (LANES, LANES)).T
    gram.middle(0)
    grad.last(0)
    gram.last(0)

    def keep_time(x):
        vt[...] = x
        high, low = halves(x)
        vcat[:rank, :] = high
        vcat[rank : 2 * rank, :] = high
        vcat[2 * rank : 3 * rank, :] = low
        vcat[3 * rank :, :] = jnp.zeros_like(low)

    def time_sum():
        return jnp.concatenate([gout[rank * j : rank * (j + 1), :] for j in range(nb)], axis=1)

    grad.end()
    keep_time(time_sum())

    def invert(first, second):
        now = vt[...]
        gram_time = exact(now, jnp.concatenate([now, now], axis=0), ((1,), (1,)))
        gram.end()
        gf = hout[...]
        gram_flow = gf + pltpu.roll(gf, rank, 1)
        lane, row = iota(gf.shape, 1), iota(gf.shape, 0)
        eye = jnp.where((lane == row) | (lane == row + rank), RIDGE, 0.0)
        a = jnp.where(lane < rank, gram_time, gram_flow) + eye
        for k in range(0, rank, 2):
            if k == FIRST_AT:
                first()
            if k == SECOND_AT:
                second()
            a = pivot(a, k, rank)
        other = pltpu.roll(a, rank, 1)
        inv_time2 = STEP * jnp.where(lane < rank, a, other)
        inv_flow[...] = STEP * other
        wt = exact(inv_time2[:, :rank], now, ((1,), (0,)))
        whi, wlo = halves(jnp.concatenate([wt, wt], axis=0).T)
        wcat[:, :LANES] = whi
        wcat[:, LANES:] = wlo
        phi, plo = halves(inv_time2)
        pcat[...] = jnp.concatenate([phi, phi, plo, jnp.zeros_like(plo)], axis=0)

    invert(lambda: None, lambda: None)
    for c in local:
        c.wait()
    for d in range(1, n_tm):
        get_traffic(d).wait_recv()
        send_traffic(d).wait_send()

    def step(it, _):
        slot, next_slot = lax.rem(it, 2), lax.rem(it + 1, 2)
        final = it == ITERS - 1
        acc[...] = jnp.zeros_like(acc)
        later = it > 0

        @pl.when(later)
        def _():
            gram.middle(slot)

        def first_tile(i, _):
            at = tile_rows(i)
            low_rank = quick(ul[at, :], vcat[...])
            limit = wide[pl.ds(pl.multiple_of(p.tm * rows + i * tile, 8), tile), :block]
            parts = []
            for j in range(n_tm):
                diff = held[j, at, :] - low_rank[:, block * j : block * (j + 1)]
                rest = jnp.minimum(jnp.maximum(diff, -limit), limit)
                parts.append(rest)

                @pl.when(final & (p.tm == j))
                def _():
                    found[pl.ds(pl.multiple_of(p.tm * rows + i * tile, 8), tile), :] = diff - rest

            rest = jnp.concatenate(parts, axis=1)
            high, low = halves(rest)
            rhi[at, :] = high
            rlo[at, :] = low
            hl = ul[at, :LANES]
            acc[...] += quick(hl, high, ((0,), (0,))) + quick(hl, low, ((0,), (0,)))
            return 0

        lax.fori_loop(0, tiles // 2, first_tile, 0)

        @pl.when(later)
        def _():
            gram.last(slot)

        lax.fori_loop(tiles // 2, tiles, first_tile, 0)
        for j in range(nb):
            cols = slice(LANES * j, LANES * (j + 1))
            gsrc[rank * j : rank * (j + 1), :] = acc[:rank, cols] + acc[rank:, cols]
        grad.begin()

        @pl.when(final)
        def _():
            send_found(p.tm).start()

        @pl.when(later)
        def _():
            invert(lambda: grad.middle(next_slot), lambda: grad.last(next_slot))

        @pl.when(jnp.logical_not(later))
        def _():
            grad.middle(next_slot)
            grad.last(next_slot)

        now = vt[...]
        gacc[...] = jnp.zeros_like(gacc)

        def second_tile(i, _):
            at = tile_rows(i)
            o = quick(rhi[at, :], wcat[...])
            o = o[:, :LANES] + o[:, LANES:] + quick(rlo[at, :], wcat[:, :LANES]) - quick(ul[at, :], pcat[...])
            keep_flow(at, u2[at, :] + o)
            return 0

        lax.fori_loop(0, tiles, second_tile, 0)

        @pl.when(jnp.logical_not(final))
        def _():
            send_gram()

        @pl.when(it == ITERS - 2)
        def _():
            upack[...] = jnp.where(iota((half, LANES), 1) < rank, u2[:half, :], u2[half:, :])
            for d in range(1, n_tm):
                send_flow(d, False).start()

        @pl.when(final)
        def _():
            mine = jnp.zeros((rank, block), F32)
            for j in range(n_tm):
                mine = jnp.where(p.tm == j, now[:, block * j : block * (j + 1)], mine)
            vhi, vlo = halves(mine)
            zero = jnp.zeros_like(vhi)
            ops = (
                (jnp.concatenate([vhi, zero, vhi, zero], axis=0), jnp.concatenate([vlo, zero], axis=0)),
                (jnp.concatenate([zero, vhi, zero, vhi], axis=0), jnp.concatenate([zero, vlo], axis=0)),
            )
            for d in range(1, n_tm):
                send_flow(d, True).wait_recv()
                peer = lax.rem(p.tm + d, n_tm)
                high, low = halves(ug[peer])
                both = jnp.concatenate([high, low], axis=1)
                for h in range(2):
                    at = pl.ds(pl.multiple_of(peer * rows + h * half, 8), half)
                    low_rank = quick(both, ops[h][0]) + quick(high, ops[h][1])
                    diff = whole[at, :] - low_rank
                    limit = wide[at, :block]
                    found[at, :] = diff - jnp.minimum(jnp.maximum(diff, -limit), limit)
                send_flow(d, False).wait_send()
                send_found(peer).start()
            flow_out[...] = u2[...].T[:rank, :]

        grad.end()
        keep_time(now + exact(inv_flow[:, :rank], time_sum() - now, ((1,), (0,))))
        return 0

    lax.fori_loop(0, ITERS, step, 0)
    stage[...] = jnp.concatenate([vt[...], vt[...]], axis=0).T
    time_out[...] = stage[pl.ds(at, share), :rank]
    for d in range(n_tm):
        send_found(lax.rem(p.tm + d, n_tm)).wait()


def solution(mesh):
    n_flow, n_tm = mesh.shape["flow"], mesh.shape["tm"]

    def body(traffic, thresholds, flow_factor, time_factor):
        all_rows, block = traffic.shape
        rows, rank = flow_factor.shape
        bins = block * n_tm
        n1 = 8
        n2 = n_flow * n_tm // n1
        gr, hr = rank * bins // LANES, rank
        thr = thresholds.reshape(all_rows // LANES, LANES)
        vmem = pl.BlockSpec(memory_space=pltpu.VMEM)
        dma = pltpu.SemaphoreType.DMA
        sums = []
        sems = []
        for r in (gr, hr):
            c = r // n1
            sums += [
                pltpu.VMEM((r, LANES), F32), pltpu.VMEM((n1, c, LANES), F32),
                pltpu.VMEM((2, n2, c, LANES), F32), pltpu.VMEM((r, LANES), F32),
            ]
            sems += [dma((n1,)), dma((n1,)), dma((n2,)), dma((2, n2)), dma((n1,)), dma((n1,))]
        anomaly, flow_new, time_new = pl.pallas_call(
            functools.partial(kernel, n_flow, n_tm),
            out_shape=(
                jax.ShapeDtypeStruct((all_rows, block), F32),
                jax.ShapeDtypeStruct((rank, rows), F32),
                jax.ShapeDtypeStruct(time_factor.shape, F32),
            ),
            in_specs=[pl.BlockSpec(memory_space=pl.ANY), vmem, vmem, vmem],
            out_specs=(pl.BlockSpec(memory_space=pl.ANY), vmem, vmem),
            scratch_shapes=[
                pltpu.VMEM((n_tm, rows, block), F32),
                pltpu.VMEM((all_rows, block), F32),
                pltpu.VMEM((all_rows, LANES), F32),
                pltpu.VMEM((rows, LANES), F32),
                pltpu.VMEM((rows, 2 * LANES), BF16),
                pltpu.VMEM((rows, bins), BF16),
                pltpu.VMEM((rows, bins), BF16),
                pltpu.VMEM((rank, bins), F32),
                pltpu.VMEM((4 * rank, bins), BF16),
                pltpu.VMEM((2 * rank, bins), F32),
                pltpu.VMEM((2 * rank, LANES), F32),
                pltpu.VMEM((bins, LANES), F32),
                pltpu.VMEM((n_tm, rows // 2, LANES), F32),
                pltpu.VMEM((rows // 2, LANES), F32),
            ] + sums + sems + [
                dma((n_tm,)), dma((n_tm,)), dma((2,)), dma((n_tm,)), dma((n_tm,)), dma((n_tm,)),
                pltpu.VMEM((all_rows, block), F32),
                pltpu.VMEM((bins, 2 * LANES), BF16),
                pltpu.VMEM((4 * rank, LANES), BF16),
                pltpu.VMEM((rank, LANES), F32),
            ],
            compiler_params=pltpu.CompilerParams(
                collective_id=0, has_side_effects=True, vmem_limit_bytes=56 * 1024 * 1024
            ),
            name="pca",
        )(traffic, thr, flow_factor.T, time_factor)
        return anomaly, flow_new.T, time_new

    return jax.shard_map(
        body,
        mesh=mesh,
        in_specs=(P("flow", "tm"), P("flow"), P(("flow", "tm"), None), P(("tm", "flow"), None)),
        out_specs=(P("flow", "tm"), P(("flow", "tm"), None), P(("tm", "flow"), None)),
        check_vma=False,
    )
```

```python
import functools
import jax
import jax.numpy as jnp
from jax import lax
from jax.experimental import pallas as pl
from jax.experimental.pallas import tpu as pltpu
from jax.sharding import PartitionSpec as P

ITERS = 4
STEP = 0.5
RIDGE = 1.0
LANES = 128
FIRST_AT = 24
SECOND_AT = 56
F32 = jnp.float32
BF16 = jnp.bfloat16
MESH = pl.DeviceIdType.MESH


def exact(a, b, dims):
    return lax.dot_general(
        a, b, (dims, ((), ())), precision=lax.Precision.HIGHEST, preferred_element_type=F32
    )


def quick(a, b, dims=((1,), (0,))):
    return lax.dot_general(a, b, (dims, ((), ())), preferred_element_type=F32)


def halves(x):
    high = x.astype(BF16)
    return high, (x - high.astype(F32)).astype(BF16)


def iota(shape, dim):
    return lax.broadcasted_iota(jnp.int32, shape, dim)


class Total:
    def __init__(self, place, source, first, second, out, sems):
        self.place, self.source, self.first, self.second, self.out = place, source, first, second, out
        self.s1, self.r1, self.s2, self.r2, self.s3, self.r3 = sems
        self.c = source.shape[0] // place.n1

    def rows(self, member):
        return pl.ds(pl.multiple_of(member * self.c, 8), self.c)

    def copy1(self, d):
        p = self.place
        peer = lax.rem(p.g1 + d, p.n1)
        return pltpu.make_async_remote_copy(
            src_ref=self.source.at[self.rows(peer)], dst_ref=self.first.at[d],
            send_sem=self.s1.at[d], recv_sem=self.r1.at[d],
            device_id=p.device(peer, p.g2), device_id_type=MESH)

    def copy2(self, d, slot, landing):
        p = self.place
        peer = lax.rem(p.g2 + d, p.n2)
        who = peer if landing else p.g2
        return pltpu.make_async_remote_copy(
            src_ref=self.second.at[slot, who], dst_ref=self.second.at[slot, who],
            send_sem=self.s2.at[d], recv_sem=self.r2.at[slot, who],
            device_id=p.device(p.g1, peer), device_id_type=MESH)

    def copy3(self, d, landing):
        p = self.place
        peer = lax.rem(p.g1 + d, p.n1)
        who = peer if landing else p.g1
        return pltpu.make_async_remote_copy(
            src_ref=self.out.at[self.rows(who)], dst_ref=self.out.at[self.rows(who)],
            send_sem=self.s3.at[d], recv_sem=self.r3.at[who],
            device_id=p.device(peer, p.g2), device_id_type=MESH)

    def begin(self):
        for d in range(1, self.place.n1):
            self.copy1(d).start()

    def middle(self, slot):
        p = self.place
        total = self.source[self.rows(p.g1), :]
        for d in range(1, p.n1):
            self.copy1(d).wait_recv()
            total = total + self.first[d]
        self.second[slot, p.g2] = total
        p.others2(lambda d: self.copy2(d, slot, False).start())
        for d in range(1, p.n1):
            self.copy1(d).wait_send()

    def last(self, slot):
        p = self.place
        p.others2(lambda d: self.copy2(d, slot, True).wait_recv())
        p.others2(lambda d: self.copy2(d, slot, False).wait_send())
        if p.n2 <= 8:
            total = self.second[slot, 0]
            for j in range(1, p.n2):
                total = total + self.second[slot, j]
        else:
            total = lax.fori_loop(
                1, p.n2, lambda j, t: t + self.second[slot, j], self.second[slot, 0])
        self.out[self.rows(p.g1), :] = total
        for d in range(1, p.n1):
            self.copy3(d, False).start()

    def end(self):
        p = self.place
        for d in range(1, p.n1):
            self.copy3(d, True).wait_recv()
        for d in range(1, p.n1):
            self.copy3(d, False).wait_send()


class Place:
    def __init__(self, n_flow, n_tm):
        self.fl, self.tl = 4, 2
        self.n1 = self.fl * self.tl
        self.th = n_tm // self.tl
        self.n2 = n_flow // self.fl * self.th
        self.n_flow, self.n_tm = n_flow, n_tm
        self.flow, self.tm = lax.axis_index("flow"), lax.axis_index("tm")
        self.g1 = lax.rem(self.flow, self.fl) * self.tl + lax.rem(self.tm, self.tl)
        self.g2 = lax.div(self.flow, self.fl) * self.th + lax.div(self.tm, self.tl)

    def device(self, g1, g2):
        return (
            lax.div(g2, self.th) * self.fl + lax.div(g1, self.tl),
            lax.rem(g2, self.th) * self.tl + lax.rem(g1, self.tl),
        )

    def others2(self, do):
        if self.n2 <= 8:
            for d in range(1, self.n2):
                do(d)
        else:
            lax.fori_loop(1, self.n2, lambda d, _: (do(d), 0)[1], 0)


def pivot(a, k, rank):
    lane, row = iota(a.shape, 1), iota(a.shape, 0)
    left = lane < rank
    own = jnp.where(left, lane, lane - rank)
    first, second = own == k, own == k + 1
    col = jnp.where(left, a[:, k : k + 1], a[:, rank + k : rank + k + 1])
    col_next = jnp.where(left, a[:, k + 1 : k + 2], a[:, rank + k + 1 : rank + k + 2])
    p, q, s = col[k : k + 1, :], col[k + 1 : k + 2, :], col_next[k + 1 : k + 2, :]
    scale = 1.0 / (p * s - q * q)
    line = jnp.where(first[:1], 1.0, jnp.where(second[:1], 0.0, a[k : k + 1, :]))
    line_next = jnp.where(first[:1], 0.0, jnp.where(second[:1], 1.0, a[k + 1 : k + 2, :]))
    out = (s * scale) * line - (q * scale) * line_next
    out_next = (p * scale) * line_next - (q * scale) * line
    col = jnp.where(row == k, -1.0, jnp.where(row == k + 1, 0.0, col))
    col_next = jnp.where(row == k, 0.0, jnp.where(row == k + 1, -1.0, col_next))
    rest = jnp.where(first | second | (row == k) | (row == k + 1), 0.0, a)
    return rest - col * out - col_next * out_next


def kernel(
    n_flow, n_tm, traffic, thr, flow_ref, time_ref, anom_out, flow_out, time_out,
    held, whole, wide, u2, ul, rhi, rlo, vt, vcat, acc, gacc, stage, ug, upack,
    gsrc, gfirst, gsecond, gout, hsrc, hfirst, hsecond, hout,
    gs1, gr1, gs2, gr2, gs3, gr3, hs1, hr1, hs2, hr2, hs3, hr3,
    tsend, trecv, tlocal, usend, urecv, asend,
    found, wcat, pcat, inv_flow,
):
    p = Place(n_flow, n_tm)
    rank = vt.shape[0]
    bins = vt.shape[1]
    rows = u2.shape[0]
    block = bins // n_tm
    half = rows // 2
    nb = bins // LANES
    tile = rows // 4 if rows % 64 == 0 else rows
    tiles = rows // tile
    grad = Total(p, gsrc, gfirst, gsecond, gout, (gs1, gr1, gs2, gr2, gs3, gr3))
    gram = Total(p, hsrc, hfirst, hsecond, hout, (hs1, hr1, hs2, hr2, hs3, hr3))

    barrier = pltpu.get_barrier_semaphore()
    for d in range(1, p.n1):
        pl.semaphore_signal(barrier, 1, device_id=p.device(lax.rem(p.g1 + d, p.n1), p.g2), device_id_type=MESH)
    p.others2(lambda d: pl.semaphore_signal(
        barrier, 1, device_id=p.device(p.g1, lax.rem(p.g2 + d, p.n2)), device_id_type=MESH))
    for d in range(1, n_tm):
        pl.semaphore_signal(barrier, 1, device_id=(p.flow, lax.rem(p.tm + d, n_tm)), device_id_type=MESH)

    def own_rows(who):
        return pl.ds(pl.multiple_of(who * rows, 8), rows)

    def send_traffic(d):
        peer = lax.rem(p.tm + d, n_tm)
        return pltpu.make_async_remote_copy(
            src_ref=traffic.at[own_rows(peer)], dst_ref=held.at[p.tm],
            send_sem=tsend.at[d], recv_sem=trecv.at[p.tm],
            device_id=(p.flow, peer), device_id_type=MESH)

    def get_traffic(d):
        peer = lax.rem(p.tm + d, n_tm)
        return pltpu.make_async_remote_copy(
            src_ref=traffic.at[own_rows(peer)], dst_ref=held.at[peer],
            send_sem=tsend.at[d], recv_sem=trecv.at[peer],
            device_id=(p.flow, peer), device_id_type=MESH)

    def send_found(who):
        return pltpu.make_async_copy(found.at[own_rows(who)], anom_out.at[own_rows(who)], asend.at[who])

    def send_flow(d, landing):
        peer = lax.rem(p.tm + d, n_tm)
        who = peer if landing else p.tm
        return pltpu.make_async_remote_copy(
            src_ref=upack, dst_ref=ug.at[who], send_sem=usend.at[d], recv_sem=urecv.at[who],
            device_id=(p.flow, peer), device_id_type=MESH)

    local = [
        pltpu.make_async_copy(traffic, whole, tlocal.at[0]),
        pltpu.make_async_copy(traffic.at[own_rows(p.tm)], held.at[p.tm], tlocal.at[1]),
    ]
    for c in local:
        c.start()

    stage[...] = jnp.zeros_like(stage)
    share = time_ref.shape[0]
    mine = p.tm * n_flow + p.flow
    at = mine * share
    if share % 8 == 0:
        at = pl.multiple_of(at, 8)
    stage[pl.ds(at, share), :rank] = time_ref[...]
    turned = stage[...].T[:rank]
    for j in range(nb):
        gsrc[rank * j : rank * (j + 1), :] = turned[:, LANES * j : LANES * (j + 1)]

    pl.semaphore_wait(barrier, p.n1 + p.n2 + n_tm - 3)
    grad.begin()

    left = iota((tile, LANES), 1) < rank

    def keep_flow(at, x):
        u2[at, :] = x
        high = x.astype(BF16)
        high32 = high.astype(F32)
        hl = jnp.where(left, high32, x - high32).astype(BF16)
        ul[at, :LANES] = hl
        ul[at, LANES:] = high
        gacc[...] += quick(hl, hl, ((0,), (0,)))

    def tile_rows(i):
        return pl.ds(pl.multiple_of(i * tile, 16), tile)

    def send_gram():
        hsrc[...] = gacc[:rank, :] + gacc[rank:, :]
        gram.begin()

    gacc[...] = jnp.zeros_like(gacc)

    u2[...] = jnp.concatenate([flow_ref[...], flow_ref[...]], axis=0).T

    def start_tile(i, _):
        keep_flow(tile_rows(i), u2[tile_rows(i), :])
        return 0

    lax.fori_loop(0, tiles, start_tile, 0)
    send_gram()
    grad.middle(0)
    for i in range(thr.shape[0]):
        wide[LANES * i : LANES * (i + 1), :] = jnp.broadcast_to(thr[i : i + 1, :], (LANES, LANES)).T
    gram.middle(0)
    grad.last(0)
    gram.last(0)
    for d in range(1, n_tm):
        send_traffic(d).start()

    def keep_time(x):
        vt[...] = x
        high, low = halves(x)
        vcat[:rank, :] = high
        vcat[rank : 2 * rank, :] = high
        vcat[2 * rank : 3 * rank, :] = low
        vcat[3 * rank :, :] = jnp.zeros_like(low)

    def time_sum():
        return jnp.concatenate([gout[rank * j : rank * (j + 1), :] for j in range(nb)], axis=1)

    grad.end()
    keep_time(time_sum())

    def invert(first, second):
        now = vt[...]
        gram_time = exact(now, jnp.concatenate([now, now], axis=0), ((1,), (1,)))
        gram.end()
        gf = hout[...]
        gram_flow = gf + pltpu.roll(gf, rank, 1)
        lane, row = iota(gf.shape, 1), iota(gf.shape, 0)
        eye = jnp.where((lane == row) | (lane == row + rank), RIDGE, 0.0)
        a = jnp.where(lane < rank, gram_time, gram_flow) + eye
        for k in range(0, rank, 2):
            if k == FIRST_AT:
                first()
            if k == SECOND_AT:
                second()
            a = pivot(a, k, rank)
        other = pltpu.roll(a, rank, 1)
        inv_time2 = STEP * jnp.where(lane < rank, a, other)
        inv_flow[...] = STEP * other
        wt = exact(inv_time2[:, :rank], now, ((1,), (0,)))
        whi, wlo = halves(jnp.concatenate([wt, wt], axis=0).T)
        wcat[:, :LANES] = whi
        wcat[:, LANES:] = wlo
        phi, plo = halves(inv_time2)
        pcat[...] = jnp.concatenate([phi, phi, plo, jnp.zeros_like(plo)], axis=0)

    invert(lambda: None, lambda: None)
    for c in local:
        c.wait()
    for d in range(1, n_tm):
        get_traffic(d).wait_recv()
        send_traffic(d).wait_send()

    def step(it, _):
        slot, next_slot = lax.rem(it, 2), lax.rem(it + 1, 2)
        final = it == ITERS - 1
        acc[...] = jnp.zeros_like(acc)
        later = it > 0

        def first_tile(i, _):
            at = tile_rows(i)
            low_rank = quick(ul[at, :], vcat[...])
            limit = wide[pl.ds(pl.multiple_of(p.tm * rows + i * tile, 8), tile), :block]
            parts = []
            for j in range(n_tm):
                diff = held[j, at, :] - low_rank[:, block * j : block * (j + 1)]
                rest = jnp.minimum(jnp.maximum(diff, -limit), limit)
                parts.append(rest)

                @pl.when(final & (p.tm == j))
                def _():
                    found[pl.ds(pl.multiple_of(p.tm * rows + i * tile, 8), tile), :] = diff - rest

            rest = jnp.concatenate(parts, axis=1)
            high, low = halves(rest)
            rhi[at, :] = high
            rlo[at, :] = low
            hl = ul[at, :LANES]
            acc[...] += quick(hl, high, ((0,), (0,))) + quick(hl, low, ((0,), (0,)))
            return 0

        lax.fori_loop(0, tiles // 2, first_tile, 0)

        @pl.when(later)
        def _():
            gram.last(slot)

        lax.fori_loop(tiles // 2, tiles, first_tile, 0)
        for j in range(nb):
            cols = slice(LANES * j, LANES * (j + 1))
            gsrc[rank * j : rank * (j + 1), :] = acc[:rank, cols] + acc[rank:, cols]
        grad.begin()

        @pl.when(final)
        def _():
            send_found(p.tm).start()

        @pl.when(later)
        def _():
            invert(lambda: grad.middle(next_slot), lambda: grad.last(next_slot))

        @pl.when(jnp.logical_not(later))
        def _():
            grad.middle(next_slot)
            grad.last(next_slot)

        now = vt[...]
        gacc[...] = jnp.zeros_like(gacc)

        def second_tile(i, _):
            at = tile_rows(i)
            o = quick(rhi[at, :], wcat[...])
            o = o[:, :LANES] + o[:, LANES:] + quick(rlo[at, :], wcat[:, :LANES]) - quick(ul[at, :], pcat[...])
            keep_flow(at, u2[at, :] + o)
            return 0

        lax.fori_loop(0, tiles, second_tile, 0)

        @pl.when(jnp.logical_not(final))
        def _():
            send_gram()

        @pl.when(it == ITERS - 2)
        def _():
            upack[...] = jnp.where(iota((half, LANES), 1) < rank, u2[:half, :], u2[half:, :])
            for d in range(1, n_tm):
                send_flow(d, False).start()

        @pl.when(final)
        def _():
            mine = jnp.zeros((rank, block), F32)
            for j in range(n_tm):
                mine = jnp.where(p.tm == j, now[:, block * j : block * (j + 1)], mine)
            vhi, vlo = halves(mine)
            zero = jnp.zeros_like(vhi)
            ops = (
                (jnp.concatenate([vhi, zero, vhi, zero], axis=0), jnp.concatenate([vlo, zero], axis=0)),
                (jnp.concatenate([zero, vhi, zero, vhi], axis=0), jnp.concatenate([zero, vlo], axis=0)),
            )
            for d in range(1, n_tm):
                send_flow(d, True).wait_recv()
                peer = lax.rem(p.tm + d, n_tm)
                high, low = halves(ug[peer])
                both = jnp.concatenate([high, low], axis=1)
                for h in range(2):
                    at = pl.ds(pl.multiple_of(peer * rows + h * half, 8), half)
                    low_rank = quick(both, ops[h][0]) + quick(high, ops[h][1])
                    diff = whole[at, :] - low_rank
                    limit = wide[at, :block]
                    found[at, :] = diff - jnp.minimum(jnp.maximum(diff, -limit), limit)
                send_flow(d, False).wait_send()
                send_found(peer).start()
            flow_out[...] = u2[...].T[:rank, :]

        grad.end()

        @pl.when(jnp.logical_not(final))
        def _():
            gram.middle(next_slot)

        keep_time(now + exact(inv_flow[:, :rank], time_sum() - now, ((1,), (0,))))
        return 0

    lax.fori_loop(0, ITERS, step, 0)
    stage[...] = jnp.concatenate([vt[...], vt[...]], axis=0).T
    time_out[...] = stage[pl.ds(at, share), :rank]
    for d in range(n_tm):
        send_found(lax.rem(p.tm + d, n_tm)).wait()


def solution(mesh):
    n_flow, n_tm = mesh.shape["flow"], mesh.shape["tm"]

    def body(traffic, thresholds, flow_factor, time_factor):
        all_rows, block = traffic.shape
        rows, rank = flow_factor.shape
        bins = block * n_tm
        n1 = 8
        n2 = n_flow * n_tm // n1
        gr, hr = rank * bins // LANES, rank
        thr = thresholds.reshape(all_rows // LANES, LANES)
        vmem = pl.BlockSpec(memory_space=pltpu.VMEM)
        dma = pltpu.SemaphoreType.DMA
        sums = []
        sems = []
        for r in (gr, hr):
            c = r // n1
            sums += [
                pltpu.VMEM((r, LANES), F32), pltpu.VMEM((n1, c, LANES), F32),
                pltpu.VMEM((2, n2, c, LANES), F32), pltpu.VMEM((r, LANES), F32),
            ]
            sems += [dma((n1,)), dma((n1,)), dma((n2,)), dma((2, n2)), dma((n1,)), dma((n1,))]
        anomaly, flow_new, time_new = pl.pallas_call(
            functools.partial(kernel, n_flow, n_tm),
            out_shape=(
                jax.ShapeDtypeStruct((all_rows, block), F32),
                jax.ShapeDtypeStruct((rank, rows), F32),
                jax.ShapeDtypeStruct(time_factor.shape, F32),
            ),
            in_specs=[pl.BlockSpec(memory_space=pl.ANY), vmem, vmem, vmem],
            out_specs=(pl.BlockSpec(memory_space=pl.ANY), vmem, vmem),
            scratch_shapes=[
                pltpu.VMEM((n_tm, rows, block), F32),
                pltpu.VMEM((all_rows, block), F32),
                pltpu.VMEM((all_rows, LANES), F32),
                pltpu.VMEM((rows, LANES), F32),
                pltpu.VMEM((rows, 2 * LANES), BF16),
                pltpu.VMEM((rows, bins), BF16),
                pltpu.VMEM((rows, bins), BF16),
                pltpu.VMEM((rank, bins), F32),
                pltpu.VMEM((4 * rank, bins), BF16),
                pltpu.VMEM((2 * rank, bins), F32),
                pltpu.VMEM((2 * rank, LANES), F32),
                pltpu.VMEM((bins, LANES), F32),
                pltpu.VMEM((n_tm, rows // 2, LANES), F32),
                pltpu.VMEM((rows // 2, LANES), F32),
            ] + sums + sems + [
                dma((n_tm,)), dma((n_tm,)), dma((2,)), dma((n_tm,)), dma((n_tm,)), dma((n_tm,)),
                pltpu.VMEM((all_rows, block), F32),
                pltpu.VMEM((bins, 2 * LANES), BF16),
                pltpu.VMEM((4 * rank, LANES), BF16),
                pltpu.VMEM((rank, LANES), F32),
            ],
            compiler_params=pltpu.CompilerParams(
                collective_id=0, has_side_effects=True, vmem_limit_bytes=56 * 1024 * 1024
            ),
            name="pca",
        )(traffic, thr, flow_factor.T, time_factor)
        return anomaly, flow_new.T, time_new

    return jax.shard_map(
        body,
        mesh=mesh,
        in_specs=(P("flow", "tm"), P("flow"), P(("flow", "tm"), None), P(("tm", "flow"), None)),
        out_specs=(P("flow", "tm"), P(("flow", "tm"), None), P(("tm", "flow"), None)),
        check_vma=False,
    )
```
